128 devices in a mesh: panel: 32 (over y, z_lo, x), pole: 4 (over z_hi, core).
Axes of the slice: x: 4, y: 4, z: 4 (z_hi: 2, z_lo: 2; z = z_hi * 2 + z_lo), core: 2. Of those that a mesh axis runs over, the one named last changes fastest.
Arguments:
- amplitudes: bfloat16 [10240, 4096], P('panel', 'pole'), may hold values from -0.75 to 0.75
- factors: float32 [2, 4096], P(None, 'pole'), may hold values from -2 to 2
Outputs:
- rmatrix: float32 [2, 10240, 10240], P(None, 'panel', 'pole')
The draws below stay inside these ranges and needn't reach their ends.
All inputs are finite; a program needn't handle non-finite values.
Results may differ from the reference program's by a relative error of at most 0.0029.
Values may be sent and summed in bfloat16 or wider, within the bound.
A program may use at most 128 MiB of HBM per device.

```python
import jax
import jax.numpy as jnp
from jax import lax

NC = 10240
ENERGIES = 2
POLES = 4096


def block_levels(key, extent, cuts, low, top_value):
    loudness, own = 1.0, jax.random.fold_in(key, 6)
    for dim, blocks in cuts:
        steps = jnp.exp(jax.random.uniform(jax.random.fold_in(own, dim), (blocks,), jnp.float32, low / len(cuts), top_value / len(cuts)))
        loudness = loudness * jnp.repeat(steps, extent[dim] // blocks).reshape([-1 if axis == dim else 1 for axis in range(len(extent))])
    return loudness


def noise(rng, dims, scale, most, pieces=(), kind=jnp.bfloat16):
    entries = jax.random.normal(rng, dims, jnp.float32) * scale
    if len(pieces) > 0:
        entries = block_levels(rng, dims, pieces, -0.22, 0.18) * entries
    return jnp.clip(entries, min=-most, max=most).astype(kind)


def setup_inputs(seed: int = 0) -> dict:
    seeds = jax.random.split(jax.random.key(seed), 3)
    return {
        "amplitudes": noise(seeds[0], (NC, POLES), (POLES ** -0.25), 0.75, ((0, 32), (1, 4))),
        "factors": jnp.clip(jax.random.uniform(seeds[1], (ENERGIES, POLES), jnp.float32, -2.0, 2.0) * block_levels(seeds[1], (ENERGIES, POLES), ((1, 4),), -0.4, 0.0), -2.0, 2.0),
    }


def reference(amplitudes, factors):
    def one_energy(factor_row):
        scaled = (amplitudes.astype(jnp.float32) * factor_row[None, :]).astype(jnp.bfloat16)
        return lax.dot_general(scaled, amplitudes, (((1,), (1,)), ((), ())), preferred_element_type=jnp.float32)
    return lax.map(one_energy, factors)
```

```python
import jax
import jax.numpy as jnp
from jax import lax
from jax.experimental import pallas as pl
from jax.experimental.pallas import tpu as pltpu
from jax.sharding import PartitionSpec as P

MESH = pl.DeviceIdType.MESH
LAST = (((1,), (1,)), ((), ()))
XFIRST = (2, 3)

U = lambda j, ms, ts=(0, 1): [("U", j, t, m) for m in ms for t in ts]
SIDES = lambda ms, ts=(0, 1): [("U", j, t, m) for t in ts for m in ms for j in (3, 1)]
ORDER = (
    [("R", "s01"), ("U", 0, 0, 0), ("U", 0, 0, 1), ("R", "12_0"), ("R", "10_1"), ("U", 0, 1, 0), ("U", 0, 1, 1)]
    + [("U", 3, 0, 0), ("U", 1, 0, 0), ("R", "12_1"), ("R", "10_0"), ("U", 3, 0, 1), ("U", 1, 0, 1)]
    + [("R", "02"), ("S", 0), ("R", "s11"), ("S", 1), ("R", "s03"), ("R", "s13")]
    + [("U", 0, 0, 2), ("U", 0, 0, 3), ("U", 0, 1, 2), ("U", 0, 1, 3)]
    + [("U", 3, 1, 0), ("U", 1, 1, 0), ("U", 3, 1, 1), ("U", 1, 1, 1)]
    + [("S", 2), ("S", 3)]
    + [("U", 3, 0, 2), ("U", 1, 0, 2), ("U", 3, 0, 3), ("U", 1, 0, 3)]
    + [("U", 2, 0, 0), ("U", 2, 1, 0)]
    + [("U", 3, 1, 2), ("U", 1, 1, 2), ("U", 3, 1, 3), ("U", 1, 1, 3)]
    + [("U", 2, 0, 1), ("U", 2, 1, 1)]
    + [("U", 2, 0, 2), ("U", 2, 1, 2), ("U", 2, 0, 3), ("U", 2, 1, 3)]
)


class Sems:
    def __init__(self):
        self.ids = {}

    def __getitem__(self, name):
        return self.ids.setdefault(name, len(self.ids))


def kernel(names, a, f, outl, outr, rows, facs, scaled, cols, acc, snd, sems):
    p, q = lax.axis_index("panel"), lax.axis_index("pole")
    x, zl, y = lax.rem(p, 4), lax.rem(lax.div(p, 4), 2), lax.div(p, 8)
    zh, c = lax.div(q, 2), lax.rem(q, 2)
    half = a.shape[0] // 2

    def device(x, y, zl, zh, c):
        return ((y * 2 + zl) * 4 + x, zh * 2 + c)

    up = 2 * c - 1
    role = lax.rem((y - (2 * zh + c)) * up + 4, 4)
    right, left = device(lax.rem(x + 1, 4), y, zl, zh, c), device(lax.rem(x + 3, 4), y, zl, zh, c)
    ahead, behind = device(x, lax.rem(y + up + 4, 4), zl, zh, c), device(x, lax.rem(y - up + 4, 4), zl, zh, c)
    sibling = device(x, y, zl, zh, 1 - c)
    partner, other = device(x, y, 1 - zl, zh, c), device(x, y, 1 - zl, 1 - zh, c)
    across, across2 = device(x, y, zl, 1 - zh, c), device(x, y, zl, 1 - zh, 1 - c)

    sem = lambda name: sems.at[names[name]]

    def to_slot(src, dst, send_name, slot_name, to):
        return pltpu.make_async_remote_copy(
            src_ref=src, dst_ref=dst, send_sem=sem(("s",) + send_name), recv_sem=sem(("r",) + slot_name),
            device_id=to, device_id_type=MESH,
        )

    barrier = pltpu.get_barrier_semaphore()
    greeted = (right, left, ahead, behind, sibling, partner, other, across, across2)
    for to in greeted:
        pl.semaphore_signal(barrier, inc=1, device_id=to, device_id_type=MESH)
    pl.semaphore_wait(barrier, len(greeted))

    finish = []

    def start(make, when=None):
        if when is None:
            make().start()
            finish.append(lambda: make().wait_send())
        else:
            pl.when(when)(lambda: make().start())
            finish.append(lambda: pl.when(when)(lambda: make().wait_send()))

    part = lambda ref, t: ref.at[pl.ds(t * half, half)]

    def source(j, t, m, root):
        if root:
            return part(a, t) if m == 0 else part(rows.at[0, m], t)
        return cols.at[j, t, m]

    def sends(j, t, m):
        every = (0, 1, 2, 3)
        out = []
        xroles = (0,) if m in XFIRST else every
        if j == 0:
            out += [(xroles, right, 3), (xroles, left, 1)]
        elif j == 3 and t == 0:
            out += [(xroles, right, 2)]
        elif j == 1 and t == 1:
            out += [(xroles, left, 2)]
        if j == 0 or m in XFIRST:
            out += [((0, 1), ahead, j), ((0,), behind, j)]
        return out

    def forward(j, t, m):
        for n, (roles, to, slot) in enumerate(sends(j, t, m)):
            def make(root, to=to, slot=slot, n=n):
                return to_slot(source(j, t, m, root), cols.at[slot, t, m], ("c", j, t, m, n), ("c", slot, t, m), to)
            if j == 0:
                if 0 in roles:
                    start(lambda make=make: make(True), role == 0)
                rest = tuple(i for i in roles if i != 0)
                if rest:
                    start(lambda make=make: make(False), (role == 1) if rest == (1,) else (role != 0))
            elif len(roles) == 4:
                start(lambda make=make: make(False))
            else:
                start(lambda make=make: make(False), (role == 0) if roles == (0,) else (role < 2))

    def wait_unit(j, t, m):
        to_slot(cols.at[j, t, m], cols.at[j, t, m], ("c", 0, 0, 0, 0), ("c", j, t, m), right).wait_recv()

    def send_unit(j, t, m):
        if j == 0:
            def root_local():
                pltpu.make_async_copy(source(0, t, m, True), cols.at[0, t, m], sem(("l", t, m))).start()
            pl.when(role == 0)(root_local)
            pl.when(role != 0)(lambda: wait_unit(j, t, m))
        else:
            wait_unit(j, t, m)
        forward(j, t, m)

    def wait_rows(w, m, t=None):
        ref = rows.at[w, m] if t is None else part(rows.at[w, m], t)
        name = ("w", w, m) if t is None else ("w", w, m, t)
        to_slot(ref, ref, ("c", 0, 0, 0, 0), name, sibling).wait_recv()

    def to_sibling(w, m):
        src = a if (w, m) == (0, 0) else rows.at[w, m]
        start(lambda: to_slot(src, rows.at[w, m + 1], ("w", w, m), ("w", w, m + 1), sibling))

    def row_event(kind):
        if kind == "s01":
            wait_rows(0, 1)
        elif kind == "12_0":
            wait_rows(1, 2, 0)
            start(lambda: to_slot(part(rows.at[1, 2], 0), part(rows.at[0, 2], 0), ("z", 0), ("w", 0, 2, 0), partner))
        elif kind == "10_1":
            wait_rows(1, 0, 1)
            start(lambda: to_slot(part(rows.at[1, 0], 1), part(rows.at[0, 2], 1), ("z", 1), ("w", 0, 2, 1), other))
        elif kind == "12_1":
            wait_rows(1, 2, 1)
            to_sibling(1, 2)
        elif kind == "10_0":
            wait_rows(1, 0, 0)
            to_sibling(1, 0)
        elif kind == "02":
            wait_rows(0, 2, 0)
            wait_rows(0, 2, 1)
            to_sibling(0, 2)
        elif kind == "s11":
            wait_rows(1, 1)
        elif kind == "s03":
            wait_rows(0, 3)
        elif kind == "s13":
            wait_rows(1, 3)

    def scale(m):
        if m:
            to_slot(facs.at[m], facs.at[m], ("c", 0, 0, 0, 0), ("f", m), sibling).wait_recv()
        fac = f if m == 0 else facs.at[m]
        energies, full, step = f.shape[0], 2 * half, 32
        for w in (0, 1):
            src = a if (w, m) == (0, 0) else rows.at[w, m]

            def body(i, _):
                at = pl.ds(pl.multiple_of(i * step, step), step)
                block = src[at, :].astype(jnp.float32)
                for e in range(energies):
                    scaled[m, w * energies + e, at, :] = (block * fac[e : e + 1, :]).astype(jnp.bfloat16)
                return 0

            lax.fori_loop(0, full // step, body, 0)

    def piece(i, j, t, w, e):
        total = None
        for m in range(4):
            term = lax.dot_general(scaled[m, w * 2 + e], cols[j, t, m], LAST, preferred_element_type=jnp.float32)
            total = term if total is None else total + term
        if w:
            snd[i, e] = total.astype(jnp.bfloat16)
        else:
            acc[i, e] = total
        if e == 1:
            column = lax.rem(x + j, 4)
            if w:
                start(lambda: to_slot(snd.at[i], outr.at[column, t], ("o", i), ("o", j, t), partner))
            else:
                local = lambda: pltpu.make_async_copy(acc.at[i], outl.at[column, t], sem(("ol", i)))
                local().start()
                finish.append(lambda: local().wait())

    def z_start(t, m, to):
        start(lambda: to_slot(part(a, t), part(rows.at[1, m], t), ("z", m, t), ("w", 1, m, t), to))

    z_start(0, 2, other)
    z_start(1, 0, partner)
    to_sibling(0, 0)
    z_start(1, 2, other)
    z_start(0, 0, partner)
    for m, to in ((1, sibling), (2, across), (3, across2)):
        start(lambda m=m, to=to: to_slot(f, facs.at[m], ("f", m), ("f", m), to))

    pending, seen, done = [], {}, 0
    scaled_ready = 0
    ready = []
    for event in ORDER:
        if event[0] == "R":
            row_event(event[1])
        elif event[0] == "S":
            scale(event[1])
            scaled_ready += 1
        else:
            _, j, t, m = event
            send_unit(j, t, m)
            seen[j, t] = seen.get((j, t), 0) + 1
            if seen[j, t] == 4:
                ready.append((j, t))
        if scaled_ready == 4:
            while ready:
                j, t = ready.pop(0)
                if j == 0:
                    for m in range(4):
                        pl.when(role == 0)(
                            lambda: pltpu.make_async_copy(source(0, t, m, True), cols.at[0, t, m], sem(("l", t, m))).wait()
                        )
                pending += [(done, j, t, w, e) for w in (1, 0) for e in (0, 1)]
                done += 1
            if pending:
                piece(*pending.pop(0))
    while pending:
        piece(*pending.pop(0))

    for j in range(4):
        for t in (0, 1):
            column = lax.rem(x + j, 4)
            to_slot(snd.at[0], outr.at[column, t], ("o", 0), ("o", j, t), partner).wait_recv()
    for wait in finish:
        wait()


def gather_and_multiply(a, f):
    n, k = a.shape
    half = n // 2
    names = Sems()
    shape = (4, 2, 2, n, half)
    bf16, f32 = jnp.bfloat16, jnp.float32
    any_ = pl.BlockSpec(memory_space=pl.ANY)
    vmem = pl.BlockSpec(memory_space=pltpu.VMEM)
    return pl.pallas_call(
        lambda *refs: kernel(names, *refs),
        out_shape=(jax.ShapeDtypeStruct(shape, f32), jax.ShapeDtypeStruct(shape, bf16)),
        in_specs=[vmem, vmem],
        out_specs=(any_, any_),
        scratch_shapes=[
            pltpu.VMEM((2, 4, n, k), bf16),
            pltpu.VMEM((4, 2, k), f32),
            pltpu.VMEM((4, 4, n, k), bf16),
            pltpu.VMEM((4, 2, 4, half, k), bf16),
            pltpu.VMEM((8, 2, n, half), f32),
            pltpu.VMEM((8, 2, n, half), bf16),
            pltpu.SemaphoreType.DMA((256,)),
        ],
        compiler_params=pltpu.CompilerParams(
            collective_id=0, has_side_effects=True, vmem_limit_bytes=52 << 20
        ),
        cost_estimate=pl.CostEstimate(flops=2 * 4 * n * 8 * half * 4 * k, bytes_accessed=8 * n * n * 16, transcendentals=0),
        name="gather_multiply",
    )(a, f)


def shards(a, f):
    n = a.shape[0]
    zl = lax.rem(lax.div(lax.axis_index("panel"), 4), 2)
    mine, theirs = gather_and_multiply(a, f)

    def flat(block):
        return jnp.transpose(block, (2, 3, 0, 1, 4)).reshape(2, n, 4 * n)

    mine, theirs = flat(mine), flat(theirs).astype(jnp.float32)
    first = jnp.where(zl == 0, mine, theirs)
    second = jnp.where(zl == 0, theirs, mine)
    return jnp.concatenate([first, second], axis=2)


def solution(mesh):
    in_specs = (P("panel", "pole"), P(None, "pole"))
    out_specs = P(None, "panel", "pole")
    return jax.shard_map(shards, mesh=mesh, in_specs=in_specs, out_specs=out_specs, check_vma=False)
```

```python
import jax
import jax.numpy as jnp
from jax import lax
from jax.experimental import pallas as pl
from jax.experimental.pallas import tpu as pltpu
from jax.sharding import PartitionSpec as P

MESH = pl.DeviceIdType.MESH
LAST = (((1,), (1,)), ((), ()))
XFIRST = ((0, 0), (0, 1), (1, 0))
ORDER = (
    ("R", "s01"), ("U", 0, 1, 0), ("P",), ("U", 0, 0, 1), ("P",), ("U", 0, 1, 1), ("Z", 0, "rest"), ("Z", 0, "root"),
    ("U", 0, 1, 3), ("U", 0, 1, 2), ("Z", 1, "rest"), ("R", "10_1"), ("Z", 1, "root"), ("U", 0, 0, 0), ("R", "10_0"),
    ("U", 0, 0, 2), ("U", 3, 1, 3), ("R", "s11"), ("R", "12_0"), ("U", 3, 1, 1), ("U", 0, 0, 3), ("R", "12_1"),
    ("R", "02"), ("P",), ("U", 1, 1, 0), ("U", 3, 1, 2), ("Y", 1, 1, 0), ("S", 1), ("S", 0), ("U", 3, 0, 0), ("P",),
    ("P",), ("S", 2), ("R", "s13"), ("Y", 3, 0, 0), ("R", "s03"), ("S", 3), ("U", 1, 0, 0), ("Y", 1, 0, 0), ("P",),
    ("P",), ("U", 1, 1, 3), ("P",), ("U", 3, 0, 1), ("Y", 3, 0, 1), ("P",), ("U", 3, 1, 0), ("U", 3, 0, 2), ("P",),
    ("Y", 3, 1, 0), ("U", 1, 1, 1), ("U", 1, 1, 2), ("U", 1, 0, 1), ("P",), ("Y", 1, 0, 1), ("U", 1, 0, 2),
    ("U", 1, 0, 3), ("U", 2, 0, 0), ("Y", 2, 0, 0), ("P",), ("P",), ("U", 2, 1, 0), ("Y", 2, 1, 0), ("U", 3, 0, 3),
    ("P",), ("P",), ("P",), ("P",), ("U", 2, 0, 1), ("Y", 2, 0, 1), ("U", 2, 0, 2), ("P",), ("P",), ("P",),
    ("U", 2, 0, 3), ("U", 2, 1, 1), ("U", 2, 1, 3), ("U", 2, 1, 2),
)

EARLY = ((2, 0), (2, 1))


class Sems:
    def __init__(self):
        self.ids = {}

    def __getitem__(self, name):
        return self.ids.setdefault(name, len(self.ids))


def kernel(names, a, f, outl, outr, rows, facs, scaled, cols, acc, early, snd, sems):
    p, q = lax.axis_index("panel"), lax.axis_index("pole")
    x, zl, y = lax.rem(p, 4), lax.rem(lax.div(p, 4), 2), lax.div(p, 8)
    zh, c = lax.div(q, 2), lax.rem(q, 2)
    half = a.shape[0] // 2

    def device(x, y, zl, zh, c):
        return ((y * 2 + zl) * 4 + x, zh * 2 + c)

    up = 2 * c - 1
    role = lax.rem((y - (2 * zh + c)) * up + 4, 4)
    right, left = device(lax.rem(x + 1, 4), y, zl, zh, c), device(lax.rem(x + 3, 4), y, zl, zh, c)
    ahead, behind = device(x, lax.rem(y + up + 4, 4), zl, zh, c), device(x, lax.rem(y - up + 4, 4), zl, zh, c)
    sibling = device(x, y, zl, zh, 1 - c)
    partner, other = device(x, y, 1 - zl, zh, c), device(x, y, 1 - zl, 1 - zh, c)
    across, across2 = device(x, y, zl, 1 - zh, c), device(x, y, zl, 1 - zh, 1 - c)

    sem = lambda name: sems.at[names[name]]

    def to_slot(src, dst, send_name, slot_name, to):
        return pltpu.make_async_remote_copy(
            src_ref=src, dst_ref=dst, send_sem=sem(("s",) + send_name), recv_sem=sem(("r",) + slot_name),
            device_id=to, device_id_type=MESH,
        )

    barrier = pltpu.get_barrier_semaphore()
    greeted = (right, left, ahead, behind, sibling, partner, other, across, across2)
    for to in greeted:
        pl.semaphore_signal(barrier, inc=1, device_id=to, device_id_type=MESH)
    pl.semaphore_wait(barrier, len(greeted))

    finish = []

    def start(make, when=None):
        if when is None:
            make().start()
            finish.append(lambda: make().wait_send())
        else:
            pl.when(when)(lambda: make().start())
            finish.append(lambda: pl.when(when)(lambda: make().wait_send()))

    part = lambda ref, t: ref.at[pl.ds(t * half, half)]

    def source(j, t, m, root):
        if root:
            return part(a, t) if m == 0 else part(rows.at[0, m], t)
        return cols.at[j, t, m]

    def sends(j, t, m):
        every = (0, 1, 2, 3)
        out = []
        xroles = (0,) if (t, m) in XFIRST else every
        if j == 0:
            out += [(xroles, right, 3, "x"), (xroles, left, 1, "x")]
        elif j == 3 and t == 0:
            out += [(xroles, right, 2, "x")]
        elif j == 1 and t == 1:
            out += [(xroles, left, 2, "x")]
        if j == 0 or (t, m) in XFIRST:
            out += [((0, 1), ahead, j, "y"), ((0,), behind, j, "y")]
        return out

    def forward(j, t, m, axes):
        for n, (roles, to, slot, axis) in enumerate(sends(j, t, m)):
            if axis not in axes:
                continue

            def make(root, to=to, slot=slot, n=n):
                return to_slot(source(j, t, m, root), cols.at[slot, t, m], ("c", j, t, m, n), ("c", slot, t, m), to)
            if j == 0:
                if 0 in roles:
                    start(lambda make=make: make(True), role == 0)
                rest = tuple(i for i in roles if i != 0)
                if rest:
                    start(lambda make=make: make(False), (role == 1) if rest == (1,) else (role != 0))
            elif len(roles) == 4:
                start(lambda make=make: make(False))
            else:
                start(lambda make=make: make(False), (role == 0) if roles == (0,) else (role < 2))

    def wait_unit(j, t, m):
        to_slot(cols.at[j, t, m], cols.at[j, t, m], ("c", 0, 0, 0, 0), ("c", j, t, m), right).wait_recv()

    def send_unit(j, t, m):
        if j == 0:
            def at_root():
                if m >= 2:
                    wait_rows(0, m, t)
                if m == 2:
                    half_to_sibling(t).start()
                pltpu.make_async_copy(source(0, t, m, True), cols.at[0, t, m], sem(("l", t, m))).start()

            pl.when(role == 0)(at_root)
            pl.when(role != 0)(lambda: wait_unit(j, t, m))
        else:
            wait_unit(j, t, m)
        forward(j, t, m, ("x",) if ("Y", j, t, m) in ORDER else ("x", "y"))

    def wait_rows(w, m, t=None):
        ref = rows.at[w, m] if t is None else part(rows.at[w, m], t)
        name = ("w", w, m) if t is None else ("w", w, m, t)
        to_slot(ref, ref, ("c", 0, 0, 0, 0), name, sibling).wait_recv()

    def to_sibling(w, m):
        src = a if (w, m) == (0, 0) else rows.at[w, m]
        start(lambda: to_slot(src, rows.at[w, m + 1], ("w", w, m), ("w", w, m + 1), sibling))

    def half_to_sibling(t):
        return to_slot(part(rows.at[0, 2], t), part(rows.at[0, 3], t), ("w", 0, 2, t), ("w", 0, 3, t), sibling)

    def is_root(zh, c):
        return (lax.div(y, 2) == zh) & (lax.rem(y, 2) == c)

    sibling_root, across_root, across2_root = is_root(zh, 1 - c), is_root(1 - zh, c), is_root(1 - zh, 1 - c)

    def row_event(kind):
        if kind == "s01":
            wait_rows(0, 1)
        elif kind == "12_0":
            wait_rows(1, 2, 0)
            start(
                lambda: to_slot(part(rows.at[1, 2], 0), part(rows.at[0, 2], 0), ("z", 0), ("w", 0, 2, 0), partner),
                role != 0,
            )
        elif kind == "10_1":
            wait_rows(1, 0, 1)
            start(
                lambda: to_slot(part(rows.at[1, 0], 1), part(rows.at[0, 2], 1), ("z", 1), ("w", 0, 2, 1), other),
                jnp.logical_not(across_root),
            )
        elif kind == "12_1":
            wait_rows(1, 2, 1)
            to_sibling(1, 2)
        elif kind == "10_0":
            wait_rows(1, 0, 0)
            to_sibling(1, 0)
        elif kind == "02":

            def elsewhere():
                for t in (0, 1):
                    wait_rows(0, 2, t)

            pl.when(role != 0)(elsewhere)
            for t in (0, 1):
                pl.when((role != 0) & jnp.logical_not(sibling_root))(lambda: half_to_sibling(t).start())
                finish.append(
                    lambda t=t: pl.when(jnp.logical_not(sibling_root))(lambda: half_to_sibling(t).wait_send())
                )
        elif kind == "s11":
            wait_rows(1, 1)
        elif kind == "s03":

            def elsewhere():
                for t in (0, 1):
                    wait_rows(0, 3, t)

            pl.when(role != 0)(elsewhere)
        elif kind == "s13":
            wait_rows(1, 3)

    def scale(m):
        if m:
            to_slot(facs.at[m], facs.at[m], ("c", 0, 0, 0, 0), ("f", m), sibling).wait_recv()
        fac = f if m == 0 else facs.at[m]
        energies, full, step = f.shape[0], 2 * half, 32
        for w in (0, 1):
            src = a if (w, m) == (0, 0) else rows.at[w, m]

            def body(i, _):
                at = pl.ds(pl.multiple_of(i * step, step), step)
                block = src[at, :].astype(jnp.float32)
                for e in range(energies):
                    scaled[m, w * energies + e, at, :] = (block * fac[e : e + 1, :]).astype(jnp.bfloat16)
                return 0

            lax.fori_loop(0, full // step, body, 0)

    def piece(i, j, t, w, e, quarters, first, last):
        total = None if first else (acc[i, e] if w == 0 else early[i, e])
        for m in quarters:
            term = lax.dot_general(scaled[m, w * 2 + e], cols[j, t, m], LAST, preferred_element_type=jnp.float32)
            total = term if total is None else total + term
        if not last:
            if w:
                early[i, e] = total
            else:
                acc[i, e] = total
            return
        if w:
            snd[i, e] = total.astype(jnp.bfloat16)
            column = lax.rem(x + j, 4)
            start(lambda: to_slot(snd.at[i, e], outr.at[column, t, e], ("o", i, e), ("o", j, t, e), partner))
        else:
            acc[i, e] = total
        if e == 1 and not w:
            column = lax.rem(x + j, 4)
            local = lambda: pltpu.make_async_copy(acc.at[i], outl.at[column, t], sem(("ol", i)))
            local().start()
            finish.append(lambda: local().wait())

    def z_start(turn, where):
        for t, m, to in ((turn, 2, other), (1 - turn, 0, partner)):
            make = lambda t=t, m=m, to=to: to_slot(
                part(a, t), part(rows.at[1, m], t), ("z", m, t), ("w", 1, m, t), to
            )
            pl.when((role == 0) if where == "root" else (role != 0))(lambda: make().start())
            if where == "root":
                finish.append(lambda make=make: make().wait_send())

    for m, to, when in ((2, across, across_root), (3, across2, across2_root)):
        for t in (0, 1):
            make = lambda m=m, to=to, t=t: to_slot(part(a, t), part(rows.at[0, m], t), ("d", m, t), ("w", 0, m, t), to)
            start(make, when)
    to_sibling(0, 0)
    for m, to in ((1, sibling), (2, across), (3, across2)):
        start(lambda m=m, to=to: to_slot(f, facs.at[m], ("f", m), ("f", m), to))

    pending, seen, number, ready, scales = [], {}, {}, [], 0
    for event in ORDER:
        if event[0] == "R":
            row_event(event[1])
        elif event[0] == "Z":
            z_start(*event[1:])
        elif event[0] == "Y":
            forward(*event[1:], ("y",))
        elif event[0] == "S":
            scale(event[1])
            scales += 1
        elif event[0] == "U":
            _, j, t, m = event
            send_unit(j, t, m)
            got = seen.setdefault((j, t), [])
            got.append(m)
            if (j, t) in EARLY:
                if len(got) == 3:
                    ready.append((j, t, tuple(got), True, False))
                elif len(got) == 4:
                    ready.append((j, t, (m,), False, True))
            elif len(got) == 4:
                ready.append((j, t, (0, 1, 2, 3), True, True))
        if event[0] in ("Y", "Z") or scales < 4:
            continue
        while ready:
            j, t, quarters, first, last = ready.pop(0)
            if j == 0:
                for m in range(4):
                    pl.when(role == 0)(
                        lambda: pltpu.make_async_copy(source(0, t, m, True), cols.at[0, t, m], sem(("l", t, m))).wait()
                    )
            i = number.setdefault((j, t), len(number))
            pending += [(i, j, t, w, e, quarters, first, last) for w in (1, 0) for e in (0, 1)]
        if pending:
            piece(*pending.pop(0))
    while pending:
        piece(*pending.pop(0))

    for j in range(4):
        for t in (0, 1):
            column = lax.rem(x + j, 4)
            for e in (0, 1):
                to_slot(snd.at[0, e], outr.at[column, t, e], ("o", 0, e), ("o", j, t, e), partner).wait_recv()
    for wait in finish:
        wait()


def gather_and_multiply(a, f):
    n, k = a.shape
    half = n // 2
    names = Sems()
    shape = (4, 2, 2, n, half)
    bf16, f32 = jnp.bfloat16, jnp.float32
    any_ = pl.BlockSpec(memory_space=pl.ANY)
    vmem = pl.BlockSpec(memory_space=pltpu.VMEM)
    return pl.pallas_call(
        lambda *refs: kernel(names, *refs),
        out_shape=(jax.ShapeDtypeStruct(shape, f32), jax.ShapeDtypeStruct(shape, bf16)),
        in_specs=[vmem, vmem],
        out_specs=(any_, any_),
        scratch_shapes=[
            pltpu.VMEM((2, 4, n, k), bf16),
            pltpu.VMEM((4, 2, k), f32),
            pltpu.VMEM((4, 4, n, k), bf16),
            pltpu.VMEM((4, 2, 4, half, k), bf16),
            pltpu.VMEM((8, 2, n, half), f32),
            pltpu.VMEM((8, 2, n, half), f32),
            pltpu.VMEM((8, 2, n, half), bf16),
            pltpu.SemaphoreType.DMA((256,)),
        ],
        compiler_params=pltpu.CompilerParams(
            collective_id=0, has_side_effects=True, vmem_limit_bytes=52 << 20
        ),
        cost_estimate=pl.CostEstimate(flops=2 * 4 * n * 8 * half * 4 * k, bytes_accessed=8 * n * n * 16, transcendentals=0),
        name="gather_multiply",
    )(a, f)


def assemble_kernel(mine, theirs, out):
    zl = lax.rem(lax.div(lax.axis_index("panel"), 4), 2)
    width = out.shape[2] // 2
    for block, at in ((mine, zl), (theirs, 1 - zl)):
        pieces = [block[x, t, 0].astype(jnp.float32) for x in range(4) for t in range(2)]
        out[0, :, pl.ds(pl.multiple_of(at * width, 128), width)] = jnp.concatenate(pieces, axis=1)


def assemble(mine, theirs):
    _, _, energies, n, half = mine.shape
    step = 80
    block = pl.BlockSpec((4, 2, 1, step, half), lambda e, i: (0, 0, e, i, 0))
    return pl.pallas_call(
        assemble_kernel,
        out_shape=jax.ShapeDtypeStruct((energies, n, 16 * half), jnp.float32),
        grid=(energies, n // step),
        in_specs=[block, block],
        out_specs=pl.BlockSpec((1, step, 16 * half), lambda e, i: (e, i, 0)),
        compiler_params=pltpu.CompilerParams(vmem_limit_bytes=56 << 20),
        name="assemble",
    )(mine, theirs)


def shards(a, f):
    return assemble(*gather_and_multiply(a, f))


def solution(mesh):
    in_specs = (P("panel", "pole"), P(None, "pole"))
    out_specs = P(None, "panel", "pole")
    return jax.shard_map(shards, mesh=mesh, in_specs=in_specs, out_specs=out_specs, check_vma=False)
```

```python
import jax
import jax.numpy as jnp
from jax import lax
from jax.experimental import pallas as pl
from jax.experimental.pallas import tpu as pltpu
from jax.sharding import PartitionSpec as P

MESH = pl.DeviceIdType.MESH
LAST = (((1,), (1,)), ((), ()))
XFIRST = ((0, 1), (1, 1), (1, 3))
ORDER = (
    ("R", "s01"), ("U", 0, 0, 0), ("P",), ("Z", 0, "rest"), ("U", 0, 1, 1), ("U", 0, 0, 1), ("P",), ("P",),
    ("U", 1, 1, 1), ("Z", 1, "rest"), ("U", 0, 1, 3), ("Z", 0, "root"), ("P",), ("Z", 1, "root"), ("U", 3, 1, 1),
    ("U", 3, 0, 0), ("U", 0, 1, 0), ("P",), ("U", 1, 0, 0), ("U", 0, 1, 2), ("U", 0, 0, 3), ("U", 2, 0, 0),
    ("Y", 1, 0, 0), ("R", "10"), ("R", "12"), ("R", "02"), ("U", 3, 1, 0), ("S", 0), ("U", 0, 0, 2), ("S", 2),
    ("R", "s11"), ("S", 1), ("U", 1, 1, 2), ("R", "s13"), ("R", "s03"), ("S", 3), ("U", 1, 1, 0), ("U", 3, 1, 2),
    ("P",), ("U", 3, 0, 1), ("Y", 3, 0, 1), ("P",), ("P",), ("Y", 3, 1, 0), ("P",), ("Y", 1, 1, 0), ("U", 1, 0, 3),
    ("U", 3, 1, 3), ("P",), ("Y", 2, 0, 0), ("P",), ("U", 3, 0, 3), ("U", 1, 1, 3), ("U", 1, 0, 2), ("Y", 3, 0, 0),
    ("P",), ("P",), ("U", 1, 0, 1), ("Y", 1, 0, 1), ("P",), ("P",), ("P",), ("U", 3, 0, 2), ("U", 2, 1, 2),
    ("U", 2, 1, 1), ("P",), ("U", 2, 1, 0), ("P",), ("U", 2, 0, 1), ("Y", 2, 0, 1), ("P",), ("U", 2, 0, 3), ("P",),
    ("U", 2, 1, 3), ("Y", 2, 1, 0), ("U", 2, 0, 2),
)

EARLY = ((2, 0), (2, 1))


class Sems:
    def __init__(self):
        self.ids = {}

    def __getitem__(self, name):
        return self.ids.setdefault(name, len(self.ids))


def pack(block, ref):
    n, width = block.shape
    groups = 128 // (width - 128)
    step = n // groups
    ref[pl.ds(0, n), :] = block[:, :128].astype(ref.dtype)
    rest = [block[g * step : (g + 1) * step, 128:] for g in range(groups)]
    ref[pl.ds(n, step), :] = jnp.concatenate(rest, axis=1).astype(ref.dtype)


def unpack(block, n, width):
    rest = width - 128
    tail = [block[n:, g * rest : (g + 1) * rest] for g in range(128 // rest)]
    return jnp.concatenate([block[:n], jnp.concatenate(tail, axis=0)], axis=1)


def kernel(names, a, f, outl, outr, rows, facs, scaled, cols, acc, early, snd, sems):
    p, q = lax.axis_index("panel"), lax.axis_index("pole")
    x, zl, y = lax.rem(p, 4), lax.rem(lax.div(p, 4), 2), lax.div(p, 8)
    zh, c = lax.div(q, 2), lax.rem(q, 2)
    half = a.shape[0] // 2

    def device(x, y, zl, zh, c):
        return ((y * 2 + zl) * 4 + x, zh * 2 + c)

    up = 2 * c - 1
    role = lax.rem((y - (2 * zh + c)) * up + 4, 4)
    right, left = device(lax.rem(x + 1, 4), y, zl, zh, c), device(lax.rem(x + 3, 4), y, zl, zh, c)
    ahead, behind = device(x, lax.rem(y + up + 4, 4), zl, zh, c), device(x, lax.rem(y - up + 4, 4), zl, zh, c)
    sibling = device(x, y, zl, zh, 1 - c)
    partner, other = device(x, y, 1 - zl, zh, c), device(x, y, 1 - zl, 1 - zh, c)
    across, across2 = device(x, y, zl, 1 - zh, c), device(x, y, zl, 1 - zh, 1 - c)

    sem = lambda name: sems.at[names[name]]

    def to_slot(src, dst, send_name, slot_name, to):
        return pltpu.make_async_remote_copy(
            src_ref=src, dst_ref=dst, send_sem=sem(("s",) + send_name), recv_sem=sem(("r",) + slot_name),
            device_id=to, device_id_type=MESH,
        )

    barrier = pltpu.get_barrier_semaphore()
    greeted = (right, left, ahead, behind, sibling, partner, other, across, across2)
    for to in greeted:
        pl.semaphore_signal(barrier, inc=1, device_id=to, device_id_type=MESH)
    pl.semaphore_wait(barrier, len(greeted))

    finish = []

    def start(make, when=None):
        if when is None:
            make().start()
            finish.append(lambda: make().wait_send())
        else:
            pl.when(when)(lambda: make().start())
            finish.append(lambda: pl.when(when)(lambda: make().wait_send()))

    part = lambda ref, t: ref.at[pl.ds(t * half, half)]

    def source(j, t, m, root):
        if root:
            return part(a, t) if m == 0 else part(rows.at[0, m], t)
        return cols.at[j, t, m]

    def sends(j, t, m):
        every = (0, 1, 2, 3)
        out = []
        xroles = (0,) if (t, m) in XFIRST else every
        if j == 0:
            out += [(xroles, right, 3, "x"), (xroles, left, 1, "x")]
        elif j == 3 and t == 0:
            out += [(xroles, right, 2, "x")]
        elif j == 1 and t == 1:
            out += [(xroles, left, 2, "x")]
        if j == 0 or (t, m) in XFIRST:
            out += [((0, 1), ahead, j, "y"), ((0,), behind, j, "y")]
        return out

    def forward(j, t, m, axes):
        for n, (roles, to, slot, axis) in enumerate(sends(j, t, m)):
            if axis not in axes:
                continue

            def make(root, to=to, slot=slot, n=n):
                return to_slot(source(j, t, m, root), cols.at[slot, t, m], ("c", j, t, m, n), ("c", slot, t, m), to)
            if j == 0:
                if 0 in roles:
                    start(lambda make=make: make(True), role == 0)
                rest = tuple(i for i in roles if i != 0)
                if rest:
                    start(lambda make=make: make(False), (role == 1) if rest == (1,) else (role != 0))
            elif len(roles) == 4:
                start(lambda make=make: make(False))
            else:
                start(lambda make=make: make(False), (role == 0) if roles == (0,) else (role < 2))

    def wait_unit(j, t, m):
        to_slot(cols.at[j, t, m], cols.at[j, t, m], ("c", 0, 0, 0, 0), ("c", j, t, m), right).wait_recv()

    def send_unit(j, t, m):
        if j == 0:
            def at_root():
                if m >= 2:
                    wait_rows(0, m, t)
                if m == 2:
                    half_to_sibling(t).start()
                pltpu.make_async_copy(source(0, t, m, True), cols.at[0, t, m], sem(("l", t, m))).start()

            pl.when(role == 0)(at_root)
            pl.when(role != 0)(lambda: wait_unit(j, t, m))
        else:
            wait_unit(j, t, m)
        forward(j, t, m, ("x",) if ("Y", j, t, m) in ORDER else ("x", "y"))

    def wait_rows(w, m, t=None):
        ref = rows.at[w, m] if t is None else part(rows.at[w, m], t)
        name = ("w", w, m) if t is None else ("w", w, m, t)
        to_slot(ref, ref, ("c", 0, 0, 0, 0), name, sibling).wait_recv()

    def to_sibling(w, m):
        src = a if (w, m) == (0, 0) else rows.at[w, m]
        start(lambda: to_slot(src, rows.at[w, m + 1], ("w", w, m), ("w", w, m + 1), sibling))

    def half_to_sibling(t):
        return to_slot(part(rows.at[0, 2], t), part(rows.at[0, 3], t), ("w", 0, 2, t), ("w", 0, 3, t), sibling)

    def is_root(zh, c):
        return (lax.div(y, 2) == zh) & (lax.rem(y, 2) == c)

    sibling_root, across_root, across2_root = is_root(zh, 1 - c), is_root(1 - zh, c), is_root(1 - zh, 1 - c)

    def row_event(kind):
        if kind == "s01":
            wait_rows(0, 1)
        elif kind == "12":
            wait_rows(1, 2)
            to_sibling(1, 2)
        elif kind == "10":
            wait_rows(1, 0)
            to_sibling(1, 0)
        elif kind == "02":

            def elsewhere():
                for t in (0, 1):
                    wait_rows(0, 2, t)

            pl.when(role != 0)(elsewhere)
            for t in (0, 1):
                pl.when((role != 0) & jnp.logical_not(sibling_root))(lambda: half_to_sibling(t).start())
                finish.append(
                    lambda t=t: pl.when(jnp.logical_not(sibling_root))(lambda: half_to_sibling(t).wait_send())
                )
        elif kind == "s11":
            wait_rows(1, 1)
        elif kind == "s03":

            def elsewhere():
                for t in (0, 1):
                    wait_rows(0, 3, t)

            pl.when(role != 0)(elsewhere)
        elif kind == "s13":
            wait_rows(1, 3)

    def scale(m):
        if m:
            to_slot(facs.at[m], facs.at[m], ("c", 0, 0, 0, 0), ("f", m), sibling).wait_recv()
        else:
            for local in own:
                local().wait()
        fac = facs.at[m]
        energies, full, step = f.shape[0], 2 * half, 32
        for w in (0, 1):
            src = rows.at[w, m]

            def body(i, _):
                at = pl.ds(pl.multiple_of(i * step, step), step)
                block = src[at, :].astype(jnp.float32)
                for e in range(energies):
                    scaled[m, w * energies + e, at, :] = (block * fac[e : e + 1, :]).astype(jnp.bfloat16)
                return 0

            lax.fori_loop(0, full // step, body, 0)

    def piece(i, j, t, w, e, quarters, first, last):
        total = None if first else early[EARLY.index((j, t)), w, e]
        for m in quarters:
            term = lax.dot_general(scaled[m, w * 2 + e], cols[j, t, m], LAST, preferred_element_type=jnp.float32)
            total = term if total is None else total + term
        if not last:
            early[EARLY.index((j, t)), w, e] = total
            return
        pack(total, snd.at[i, e] if w else acc.at[i, e])
        if w:
            column = lax.rem(x + j, 4)
            start(lambda: to_slot(snd.at[i, e], outr.at[column, t, e], ("o", i, e), ("o", j, t, e), partner))
        elif e == 1:
            column = lax.rem(x + j, 4)
            local = lambda: pltpu.make_async_copy(acc.at[i], outl.at[column, t], sem(("ol", i)))
            local().start()
            finish.append(lambda: local().wait())

    own = (
        lambda: pltpu.make_async_copy(a, rows.at[0, 0], sem(("own", 0))),
        lambda: pltpu.make_async_copy(f, facs.at[0], sem(("own", 1))),
    )
    for local in own:
        local().start()
    def far(m, t, to):
        return to_slot(part(a, t), part(rows.at[0, m], t), ("d", m, t), ("w", 0, m, t), to)

    def z_start(turn, where):
        here = (role == 0) if where == "root" else (role != 0)
        if turn == 0:
            makes = [
                lambda m=m, to=to: to_slot(a, rows.at[1, m], ("z", m), ("w", 1, m), to)
                for m, to in ((2, other), (0, partner))
            ]
        else:
            makes = [lambda t=t: far(2, t, across) for t in (0, 1)]
            here = here & jnp.logical_not(across_root)
        for make in makes:
            pl.when(here)(lambda: make().start())
            if where == "root":
                finish.append(lambda make=make: make().wait_send())

    for t in (0, 1):
        pl.when(across_root)(lambda: far(2, t, across).start())
    for t in (0, 1):
        start(lambda t=t: far(3, t, across2), across2_root)
    to_sibling(0, 0)
    for m, to in ((1, sibling), (2, across), (3, across2)):
        start(lambda m=m, to=to: to_slot(f, facs.at[m], ("f", m), ("f", m), to))

    pending, seen, number, ready, scales = [], {}, {}, [], 0
    for event in ORDER:
        if event[0] == "R":
            row_event(event[1])
        elif event[0] == "Z":
            z_start(*event[1:])
        elif event[0] == "Y":
            forward(*event[1:], ("y",))
        elif event[0] == "S":
            scale(event[1])
            scales += 1
        elif event[0] == "U":
            _, j, t, m = event
            send_unit(j, t, m)
            got = seen.setdefault((j, t), [])
            got.append(m)
            if (j, t) in EARLY:
                if len(got) == 3:
                    ready.append((j, t, tuple(got), True, False))
                elif len(got) == 4:
                    ready.append((j, t, (m,), False, True))
            elif len(got) == 4:
                ready.append((j, t, (0, 1, 2, 3), True, True))
        if event[0] in ("Y", "Z") or scales < 4:
            continue
        while ready:
            j, t, quarters, first, last = ready.pop(0)
            if j == 0:
                for m in range(4):
                    pl.when(role == 0)(
                        lambda: pltpu.make_async_copy(source(0, t, m, True), cols.at[0, t, m], sem(("l", t, m))).wait()
                    )
            i = number.setdefault((j, t), len(number))
            pending += [(i, j, t, w, e, quarters, first, last) for w in (1, 0) for e in (0, 1)]
        if pending:
            piece(*pending.pop(0))
    while pending:
        piece(*pending.pop(0))

    for j in range(4):
        for t in (0, 1):
            column = lax.rem(x + j, 4)
            for e in (0, 1):
                to_slot(snd.at[0, e], outr.at[column, t, e], ("o", 0, e), ("o", j, t, e), partner).wait_recv()
    for wait in finish:
        wait()


def gather_and_multiply(a, f):
    n, k = a.shape
    half = n // 2
    names = Sems()
    shape = (4, 2, 2, n * half // 128, 128)
    bf16, f32 = jnp.bfloat16, jnp.float32
    any_ = pl.BlockSpec(memory_space=pl.ANY)
    return pl.pallas_call(
        lambda *refs: kernel(names, *refs),
        out_shape=(jax.ShapeDtypeStruct(shape, f32), jax.ShapeDtypeStruct(shape, bf16)),
        in_specs=[any_, any_],
        out_specs=(any_, any_),
        scratch_shapes=[
            pltpu.VMEM((2, 4, n, k), bf16),
            pltpu.VMEM((4, 2, k), f32),
            pltpu.VMEM((4, 4, n, k), bf16),
            pltpu.VMEM((4, 2, 4, half, k), bf16),
            pltpu.VMEM((8,) + shape[2:], f32),
            pltpu.VMEM((len(EARLY), 2, 2, n, half), f32),
            pltpu.VMEM((8,) + shape[2:], bf16),
            pltpu.SemaphoreType.DMA((256,)),
        ],
        compiler_params=pltpu.CompilerParams(
            collective_id=0, has_side_effects=True, vmem_limit_bytes=60 << 20
        ),
        cost_estimate=pl.CostEstimate(flops=2 * 4 * n * 8 * half * 4 * k, bytes_accessed=8 * n * n * 16, transcendentals=0),
        name="gather_multiply",
    )(a, f)


def assemble_kernel(n, width, mine, theirs, out, mine_in, theirs_in, blocks, in_sems, out_sems):
    zl = lax.rem(lax.div(lax.axis_index("panel"), 4), 2)
    turns = [(e, pair, kind) for e in (0, 1) for pair in (0, 1) for kind in (0, 1)]

    def fetch(i):
        e, pair, kind = turns[i]
        src, dst = (mine, mine_in) if kind == 0 else (theirs, theirs_in)
        at = pl.ds(2 * pair, 2)
        return pltpu.make_async_copy(src.at[at, :, e], dst.at[e, pair], in_sems.at[i])

    def leave(i):
        e, pair, kind = turns[i]
        side = zl if kind == 0 else 1 - zl
        at = pl.ds(pl.multiple_of((side * 2 + pair) * 4 * width, 128), 4 * width)
        return pltpu.make_async_copy(blocks.at[i], out.at[e, :, at], out_sems.at[i])

    for i in range(len(turns)):
        fetch(i).start()
    for i, (e, pair, kind) in enumerate(turns):
        fetch(i).wait()
        block = (mine_in if kind == 0 else theirs_in).at[e, pair]
        pieces = [unpack(block[x, t].astype(jnp.float32), n, width) for x in (0, 1) for t in (0, 1)]
        blocks[i] = jnp.concatenate(pieces, axis=1)
        leave(i).start()
    for i in range(len(turns)):
        leave(i).wait()


def assemble(mine, theirs, n, width):
    any_ = pl.BlockSpec(memory_space=pl.ANY)
    block = (2, 2, 2, 2) + mine.shape[3:]
    return pl.pallas_call(
        lambda *refs: assemble_kernel(n, width, *refs),
        out_shape=jax.ShapeDtypeStruct((2, n, 16 * width), jnp.float32),
        in_specs=[any_, any_],
        out_specs=any_,
        scratch_shapes=[
            pltpu.VMEM(block, jnp.float32),
            pltpu.VMEM(block, jnp.bfloat16),
            pltpu.VMEM((8, n, 4 * width), jnp.float32),
            pltpu.SemaphoreType.DMA((8,)),
            pltpu.SemaphoreType.DMA((8,)),
        ],
        compiler_params=pltpu.CompilerParams(vmem_limit_bytes=56 << 20),
        name="assemble",
    )(mine, theirs)


def shards(a, f):
    return assemble(*gather_and_multiply(a, f), a.shape[0], a.shape[0] // 2)


def solution(mesh):
    in_specs = (P("panel", "pole"), P(None, "pole"))
    out_specs = P(None, "panel", "pole")
    return jax.shard_map(shards, mesh=mesh, in_specs=in_specs, out_specs=out_specs, check_vma=False)
```

```python
import jax
import jax.numpy as jnp
from jax import lax
from jax.experimental import pallas as pl
from jax.experimental.pallas import tpu as pltpu
from jax.sharding import PartitionSpec as P

MESH = pl.DeviceIdType.MESH
LAST = (((1,), (1,)), ((), ()))
XFIRST = ((1, 1), (1, 2), (1, 3))
ORDER = (
    ("R", "s01"), ("U", 0, 0, 0), ("Z", 0, "far"), ("Z", 1, "far"), ("Z", 0, "root"), ("U", 0, 1, 0),
    ("Z", 0, "side"), ("U", 0, 1, 1), ("U", 1, 0, 0), ("Z", 1, "side"), ("P",), ("Y", 1, 0, 0), ("U", 0, 1, 2),
    ("U", 0, 1, 3), ("R", "10"), ("Z", 1, "root"), ("U", 0, 0, 1), ("U", 0, 0, 2), ("U", 0, 0, 3), ("P",), ("P",),
    ("R", "12"), ("R", "02"), ("U", 3, 1, 2), ("U", 3, 0, 1), ("P",), ("R", "s03"), ("P",), ("U", 1, 1, 0), ("P",),
    ("S", 2), ("S", 0), ("U", 3, 1, 0), ("Y", 1, 1, 0), ("P",), ("P",), ("R", "s11"), ("S", 1), ("Y", 3, 0, 1),
    ("R", "s13"), ("U", 3, 1, 1), ("S", 3), ("U", 1, 0, 2), ("U", 1, 0, 1), ("P",), ("U", 1, 1, 2), ("P",), ("P",),
    ("U", 1, 0, 3), ("U", 1, 1, 3), ("P",), ("U", 3, 0, 0), ("P",), ("U", 3, 1, 3), ("Y", 1, 0, 1), ("Y", 3, 0, 0),
    ("P",), ("U", 2, 1, 0), ("P",), ("U", 1, 1, 1), ("P",), ("Y", 3, 1, 0), ("U", 3, 0, 3), ("U", 3, 0, 2),
    ("U", 2, 1, 2), ("Y", 2, 1, 0), ("P",), ("U", 2, 0, 0), ("U", 2, 0, 1), ("Y", 2, 0, 0), ("U", 2, 1, 3), ("P",),
    ("P",), ("P",), ("U", 2, 0, 3), ("U", 2, 1, 1), ("Y", 2, 0, 1), ("U", 2, 0, 2),
)

EARLY = ((2, 0), (2, 1))


class Sems:
    def __init__(self):
        self.ids = {}

    def __getitem__(self, name):
        return self.ids.setdefault(name, len(self.ids))


def pack(block, ref):
    n, width = block.shape
    groups = 128 // (width - 128)
    step = n // groups
    ref[pl.ds(0, n), :] = block[:, :128].astype(ref.dtype)
    rest = [block[g * step : (g + 1) * step, 128:] for g in range(groups)]
    ref[pl.ds(n, step), :] = jnp.concatenate(rest, axis=1).astype(ref.dtype)


def unpack(block, n, width):
    rest = width - 128
    tail = [block[n:, g * rest : (g + 1) * rest] for g in range(128 // rest)]
    return jnp.concatenate([block[:n], jnp.concatenate(tail, axis=0)], axis=1)


def kernel(names, a, f, outl, outr, rows, facs, scaled, cols, acc, early, snd, sems):
    p, q = lax.axis_index("panel"), lax.axis_index("pole")
    x, zl, y = lax.rem(p, 4), lax.rem(lax.div(p, 4), 2), lax.div(p, 8)
    zh, c = lax.div(q, 2), lax.rem(q, 2)
    half = a.shape[0] // 2

    def device(x, y, zl, zh, c):
        return ((y * 2 + zl) * 4 + x, zh * 2 + c)

    up = 2 * c - 1
    role = lax.rem((y - (2 * zh + c)) * up + 4, 4)
    right, left = device(lax.rem(x + 1, 4), y, zl, zh, c), device(lax.rem(x + 3, 4), y, zl, zh, c)
    ahead, behind = device(x, lax.rem(y + up + 4, 4), zl, zh, c), device(x, lax.rem(y - up + 4, 4), zl, zh, c)
    sibling = device(x, y, zl, zh, 1 - c)
    partner, other = device(x, y, 1 - zl, zh, c), device(x, y, 1 - zl, 1 - zh, c)
    across, across2 = device(x, y, zl, 1 - zh, c), device(x, y, zl, 1 - zh, 1 - c)

    sem = lambda name: sems.at[names[name]]

    def to_slot(src, dst, send_name, slot_name, to):
        return pltpu.make_async_remote_copy(
            src_ref=src, dst_ref=dst, send_sem=sem(("s",) + send_name), recv_sem=sem(("r",) + slot_name),
            device_id=to, device_id_type=MESH,
        )

    barrier = pltpu.get_barrier_semaphore()
    greeted = (right, left, ahead, behind, sibling, partner, other, across, across2)
    for to in greeted:
        pl.semaphore_signal(barrier, inc=1, device_id=to, device_id_type=MESH)
    pl.semaphore_wait(barrier, len(greeted))

    finish = []

    def start(make, when=None):
        if when is None:
            make().start()
            finish.append(lambda: make().wait_send())
        else:
            pl.when(when)(lambda: make().start())
            finish.append(lambda: pl.when(when)(lambda: make().wait_send()))

    part = lambda ref, t: ref.at[pl.ds(t * half, half)]

    def source(j, t, m, root):
        if root:
            return part(a, t) if m == 0 else part(rows.at[0, m], t)
        return cols.at[j, t, m]

    def sends(j, t, m):
        every = (0, 1, 2, 3)
        out = []
        xroles = (0,) if (t, m) in XFIRST else every
        if j == 0:
            out += [(xroles, right, 3, "x"), (xroles, left, 1, "x")]
        elif j == 3 and t == 0:
            out += [(xroles, right, 2, "x")]
        elif j == 1 and t == 1:
            out += [(xroles, left, 2, "x")]
        if j == 0 or (t, m) in XFIRST:
            out += [((0, 1), ahead, j, "y"), ((0,), behind, j, "y")]
        return out

    def forward(j, t, m, axes):
        for n, (roles, to, slot, axis) in enumerate(sends(j, t, m)):
            if axis not in axes:
                continue

            def make(root, to=to, slot=slot, n=n):
                return to_slot(source(j, t, m, root), cols.at[slot, t, m], ("c", j, t, m, n), ("c", slot, t, m), to)
            if j == 0:
                if 0 in roles:
                    start(lambda make=make: make(True), role == 0)
                rest = tuple(i for i in roles if i != 0)
                if rest:
                    start(lambda make=make: make(False), (role == 1) if rest == (1,) else (role != 0))
            elif len(roles) == 4:
                start(lambda make=make: make(False))
            else:
                start(lambda make=make: make(False), (role == 0) if roles == (0,) else (role < 2))

    def wait_unit(j, t, m):
        to_slot(cols.at[j, t, m], cols.at[j, t, m], ("c", 0, 0, 0, 0), ("c", j, t, m), right).wait_recv()

    def send_unit(j, t, m):
        if j == 0:
            def at_root():
                if m >= 2:
                    wait_rows(0, m, t)
                if m == 2:
                    half_to_sibling(t).start()
                pltpu.make_async_copy(source(0, t, m, True), cols.at[0, t, m], sem(("l", t, m))).start()

            pl.when(role == 0)(at_root)
            pl.when(role != 0)(lambda: wait_unit(j, t, m))
        else:
            wait_unit(j, t, m)
        forward(j, t, m, ("x",) if ("Y", j, t, m) in ORDER else ("x", "y"))

    def wait_rows(w, m, t=None):
        ref = rows.at[w, m] if t is None else part(rows.at[w, m], t)
        name = ("w", w, m) if t is None else ("w", w, m, t)
        to_slot(ref, ref, ("c", 0, 0, 0, 0), name, sibling).wait_recv()

    def to_sibling(w, m):
        src = a if (w, m) == (0, 0) else rows.at[w, m]
        start(lambda: to_slot(src, rows.at[w, m + 1], ("w", w, m), ("w", w, m + 1), sibling))

    def half_to_sibling(t):
        return to_slot(part(rows.at[0, 2], t), part(rows.at[0, 3], t), ("w", 0, 2, t), ("w", 0, 3, t), sibling)

    def is_root(zh, c):
        return (lax.div(y, 2) == zh) & (lax.rem(y, 2) == c)

    sibling_root, across_root, across2_root = is_root(zh, 1 - c), is_root(1 - zh, c), is_root(1 - zh, 1 - c)

    def row_event(kind):
        if kind == "s01":
            wait_rows(0, 1)
        elif kind == "12":
            wait_rows(1, 2)
            to_sibling(1, 2)
        elif kind == "10":
            wait_rows(1, 0)
            to_sibling(1, 0)
        elif kind == "02":

            def elsewhere():
                for t in (0, 1):
                    wait_rows(0, 2, t)

            pl.when(role != 0)(elsewhere)
            for t in (0, 1):
                pl.when((role != 0) & jnp.logical_not(sibling_root))(lambda: half_to_sibling(t).start())
                finish.append(
                    lambda t=t: pl.when(jnp.logical_not(sibling_root))(lambda: half_to_sibling(t).wait_send())
                )
        elif kind == "s11":
            wait_rows(1, 1)
        elif kind == "s03":

            def elsewhere():
                for t in (0, 1):
                    wait_rows(0, 3, t)

            pl.when(role != 0)(elsewhere)
        elif kind == "s13":
            wait_rows(1, 3)

    def scale(m):
        if m:
            to_slot(facs.at[m], facs.at[m], ("c", 0, 0, 0, 0), ("f", m), sibling).wait_recv()
        else:
            for local in own:
                local().wait()
        fac = facs.at[m]
        energies, full, step = f.shape[0], 2 * half, 32
        for w in (0, 1):
            src = rows.at[w, m]

            def body(i, _):
                at = pl.ds(pl.multiple_of(i * step, step), step)
                block = src[at, :].astype(jnp.float32)
                for e in range(energies):
                    scaled[m, w * energies + e, at, :] = (block * fac[e : e + 1, :]).astype(jnp.bfloat16)
                return 0

            lax.fori_loop(0, full // step, body, 0)

    def piece(i, j, t, w, e, quarters, first, last):
        total = None if first else early[EARLY.index((j, t)), w, e]
        for m in quarters:
            term = lax.dot_general(scaled[m, w * 2 + e], cols[j, t, m], LAST, preferred_element_type=jnp.float32)
            total = term if total is None else total + term
        if not last:
            early[EARLY.index((j, t)), w, e] = total
            return
        pack(total, snd.at[i, e] if w else acc.at[i, e])
        if w:
            column = lax.rem(x + j, 4)
            start(lambda: to_slot(snd.at[i, e], outr.at[column, t, e], ("o", i, e), ("o", j, t, e), partner))
        elif e == 1:
            column = lax.rem(x + j, 4)
            local = lambda: pltpu.make_async_copy(acc.at[i], outl.at[column, t], sem(("ol", i)))
            local().start()
            finish.append(lambda: local().wait())

    own = (
        lambda: pltpu.make_async_copy(a, rows.at[0, 0], sem(("own", 0))),
        lambda: pltpu.make_async_copy(f, facs.at[0], sem(("own", 1))),
    )
    for local in own:
        local().start()
    def far(m, t, to):
        return to_slot(part(a, t), part(rows.at[0, m], t), ("d", m, t), ("w", 0, m, t), to)

    def z_start(turn, where):
        here = {"root": role == 0, "side": role == 3, "far": (role == 1) | (role == 2)}[where]
        if turn == 0:
            makes = [
                lambda m=m, to=to: to_slot(a, rows.at[1, m], ("z", m), ("w", 1, m), to)
                for m, to in ((2, other), (0, partner))
            ]
        else:
            makes = [lambda t=t: far(2, t, across) for t in (0, 1)]
            here = here & jnp.logical_not(across_root)
        for make in makes:
            pl.when(here)(lambda: make().start())
            if where == "root":
                finish.append(lambda make=make: make().wait_send())

    for t in (0, 1):
        pl.when(across_root)(lambda: far(2, t, across).start())
    for t in (0, 1):
        start(lambda t=t: far(3, t, across2), across2_root)
    to_sibling(0, 0)
    for m, to in ((1, sibling), (2, across), (3, across2)):
        start(lambda m=m, to=to: to_slot(f, facs.at[m], ("f", m), ("f", m), to))

    def next_piece():
        at = next((n for n, p in enumerate(pending) if p[3] == 1), 0)
        piece(*pending.pop(at))

    pending, seen, number, ready, scales = [], {}, {}, [], 0
    for event in ORDER:
        if event[0] == "R":
            row_event(event[1])
        elif event[0] == "Z":
            z_start(*event[1:])
        elif event[0] == "Y":
            forward(*event[1:], ("y",))
        elif event[0] == "S":
            scale(event[1])
            scales += 1
        elif event[0] == "U":
            _, j, t, m = event
            send_unit(j, t, m)
            got = seen.setdefault((j, t), [])
            got.append(m)
            if (j, t) in EARLY:
                if len(got) == 3:
                    ready.append((j, t, tuple(got), True, False))
                elif len(got) == 4:
                    ready.append((j, t, (m,), False, True))
            elif len(got) == 4:
                ready.append((j, t, (0, 1, 2, 3), True, True))
        if event[0] in ("Y", "Z") or scales < 4:
            continue
        while ready:
            j, t, quarters, first, last = ready.pop(0)
            if j == 0:
                for m in range(4):
                    pl.when(role == 0)(
                        lambda: pltpu.make_async_copy(source(0, t, m, True), cols.at[0, t, m], sem(("l", t, m))).wait()
                    )
            i = number.setdefault((j, t), len(number))
            pending += [(i, j, t, w, e, quarters, first, last) for w in (1, 0) for e in (0, 1)]
        if pending:
            next_piece()
    while pending:
        next_piece()

    for j in range(4):
        for t in (0, 1):
            column = lax.rem(x + j, 4)
            for e in (0, 1):
                to_slot(snd.at[0, e], outr.at[column, t, e], ("o", 0, e), ("o", j, t, e), partner).wait_recv()
    for wait in finish:
        wait()


def gather_and_multiply(a, f):
    n, k = a.shape
    half = n // 2
    names = Sems()
    shape = (4, 2, 2, n * half // 128, 128)
    bf16, f32 = jnp.bfloat16, jnp.float32
    any_ = pl.BlockSpec(memory_space=pl.ANY)
    return pl.pallas_call(
        lambda *refs: kernel(names, *refs),
        out_shape=(jax.ShapeDtypeStruct(shape, f32), jax.ShapeDtypeStruct(shape, bf16)),
        in_specs=[any_, any_],
        out_specs=(any_, any_),
        scratch_shapes=[
            pltpu.VMEM((2, 4, n, k), bf16),
            pltpu.VMEM((4, 2, k), f32),
            pltpu.VMEM((4, 4, n, k), bf16),
            pltpu.VMEM((4, 2, 4, half, k), bf16),
            pltpu.VMEM((8,) + shape[2:], f32),
            pltpu.VMEM((len(EARLY), 2, 2, n, half), f32),
            pltpu.VMEM((8,) + shape[2:], bf16),
            pltpu.SemaphoreType.DMA((256,)),
        ],
        compiler_params=pltpu.CompilerParams(
            collective_id=0, has_side_effects=True, vmem_limit_bytes=60 << 20
        ),
        cost_estimate=pl.CostEstimate(flops=2 * 4 * n * 8 * half * 4 * k, bytes_accessed=8 * n * n * 16, transcendentals=0),
        name="gather_multiply",
    )(a, f)


def assemble_kernel(n, width, mine, theirs, out, mine_in, theirs_in, blocks, in_sems, out_sems):
    zl = lax.rem(lax.div(lax.axis_index("panel"), 4), 2)
    turns = [(e, pair, kind) for e in (0, 1) for pair in (0, 1) for kind in (0, 1)]

    def fetch(i):
        e, pair, kind = turns[i]
        src, dst = (mine, mine_in) if kind == 0 else (theirs, theirs_in)
        at = pl.ds(2 * pair, 2)
        return pltpu.make_async_copy(src.at[at, :, e], dst.at[e, pair], in_sems.at[i])

    def leave(i):
        e, pair, kind = turns[i]
        side = zl if kind == 0 else 1 - zl
        at = pl.ds(pl.multiple_of((side * 2 + pair) * 4 * width, 128), 4 * width)
        return pltpu.make_async_copy(blocks.at[i], out.at[e, :, at], out_sems.at[i])

    for i in range(len(turns)):
        fetch(i).start()
    for i, (e, pair, kind) in enumerate(turns):
        fetch(i).wait()
        block = (mine_in if kind == 0 else theirs_in).at[e, pair]
        pieces = [unpack(block[x, t].astype(jnp.float32), n, width) for x in (0, 1) for t in (0, 1)]
        blocks[i] = jnp.concatenate(pieces, axis=1)
        leave(i).start()
    for i in range(len(turns)):
        leave(i).wait()


def assemble(mine, theirs, n, width):
    any_ = pl.BlockSpec(memory_space=pl.ANY)
    block = (2, 2, 2, 2) + mine.shape[3:]
    return pl.pallas_call(
        lambda *refs: assemble_kernel(n, width, *refs),
        out_shape=jax.ShapeDtypeStruct((2, n, 16 * width), jnp.float32),
        in_specs=[any_, any_],
        out_specs=any_,
        scratch_shapes=[
            pltpu.VMEM(block, jnp.float32),
            pltpu.VMEM(block, jnp.bfloat16),
            pltpu.VMEM((8, n, 4 * width), jnp.float32),
            pltpu.SemaphoreType.DMA((8,)),
            pltpu.SemaphoreType.DMA((8,)),
        ],
        compiler_params=pltpu.CompilerParams(vmem_limit_bytes=56 << 20),
        name="assemble",
    )(mine, theirs)


def shards(a, f):
    return assemble(*gather_and_multiply(a, f), a.shape[0], a.shape[0] // 2)


def solution(mesh):
    in_specs = (P("panel", "pole"), P(None, "pole"))
    out_specs = P(None, "panel", "pole")
    return jax.shard_map(shards, mesh=mesh, in_specs=in_specs, out_specs=out_specs, check_vma=False)
```
